32 devices in a mesh: grp: 2 (over y), gx: 4 (over z), gy: 4 (over x, core).
Axes of the slice: x: 2, y: 2, z: 4, core: 2. Of those that a mesh axis runs over, the one named last changes fastest.
Arguments:
- output_gradient: bfloat16 [2048, 10240], P(('grp', 'gx'), 'gy'), parts along dimension 0, may hold values from -6 to 6
- normed_layer_input: bfloat16 [2048, 8192], P(('grp', 'gy'), 'gx'), parts along dimension 0, may hold values from -0.29882812 to 0.29882812
- adapter_hidden: bfloat16 [2048, 64], P(('grp', 'gx')), parts along dimension 0, may hold values from -0.29882812 to 0.29882812
- query_key_value_weight: bfloat16 [8192, 10240], P('gx', 'gy'), may hold values from -0.0625 to 0.0625
- adapter_down_factor: bfloat16 [8, 64, 8192], P('grp', None, 'gx'), parts along dimension 0, may hold values from -0.375 to 0.375
- adapter_up_factor: bfloat16 [8, 64, 10240], P('grp', None, 'gy'), parts along dimension 0, may hold values from -0.0625 to 0.0625
- block_adapter_table: int32 [128, 1], P(('grp', 'gx')), parts along dimension 0, may hold values from 0 to 3; in each aligned block of 16 rows (0 to 15, 16 to 31, ...) at most 8 rows name the same one
- block_live_rows: int32 [128], P(('grp', 'gx')), parts along dimension 0, may hold values from 1 to 16, as said below
Outputs:
- input_gradient: bfloat16 [2048, 8192], P(('grp', 'gy'), 'gx'), parts along dimension 0
- down_gradient: float32 [8, 64, 8192], P(('grp', 'gy'), None, 'gx'), parts along dimension 0
- up_gradient: float32 [8, 64, 10240], P(('grp', 'gx'), None, 'gy'), parts along dimension 0
The draws below stay inside these ranges and needn't reach their ends.
There are 2 independent parts, one for each index of `grp`. The reference program is written for one: setup_inputs(seed, part) draws one part's arguments, and reference() takes and returns one part's arrays. A program takes and returns all parts, laid end to end along the dimension named above; an argument that names none is the same for every part. Nothing has to cross between parts.
Inputs may be any that keep to these rules, and one draw needn't show every extreme that they name: `block_adapter_table`: among the 16 blocks of one index of gx no adapter is named by more than 8 blocks; every adapter names some block. `block_live_rows`: rows of a block past its count are padding; the first block of each index of gx is full.
All inputs are finite; a program needn't handle non-finite values.
Results may differ from the reference program's by a relative error of at most 0.012.
Values may be sent and summed in bfloat16 or wider, within the bound.
A program may use at most 128 MiB of HBM per device.

```python
import math
import jax
import jax.numpy as jnp
import numpy as np
from jax import lax

MODEL_WIDTH = 8192
JOINED_WIDTH = 10240
ADAPTER_RANK = 64
BLOCK_ROWS = 16
TOK_DEV = 256
TOKEN_ROWS = 1024
BPD = 16
BLOCK_COUNT = 64
ADAPTER_COUNT = 4
CAP = 8
N_GY = 4


def draw_block_live_rows(key, part):
    key = jax.random.fold_in(key, 11)
    counts = jax.random.randint(key, (BLOCK_COUNT,), 1, BLOCK_ROWS + 1, dtype=jnp.int32)
    full_block = jnp.arange(BLOCK_COUNT, dtype=jnp.int32) % (TOK_DEV // BLOCK_ROWS) == 0
    return jnp.where(full_block, BLOCK_ROWS, counts).astype(jnp.int32)


def block_scale(stream_key, shape, pieces, least, high):
    loudness = 1.0
    for position, parts in pieces:
        heights = jax.random.uniform(jax.random.fold_in(jax.random.fold_in(stream_key, 6), position), (parts,), jnp.float32, least / len(pieces), high / len(pieces))
        loudness = loudness * jnp.repeat(jnp.exp(heights), shape[position] // parts).reshape((-1,) + (1,) * (len(shape) - 1 - position))
    return loudness


def shared_out(rng, own, number, rows, amount, top, bound, lean):
    order = jax.random.permutation(rng, amount)
    heavy_load, ordinary = shares(amount, rows * top, bound, lean, True), shares(amount, rows * top, bound, lean, False)
    places = jnp.arange(amount)

    def named(lengths, rotation):
        used = int((lengths > 0).sum())
        fixed = max(1, used // 4)
        passed = fixed + (places - fixed + rotation * (used - fixed)) % max(1, amount - fixed)
        return jnp.zeros((amount,), jnp.int32).at[order[jnp.where(places < fixed, places, passed)]].set(jnp.asarray(lengths, jnp.int32))

    lengths = jnp.where(number % 4 == 0, named(heavy_load, number // 4), named(ordinary, number - number // 4 - 1))
    mixed = jax.random.permutation(jax.random.fold_in(own, 3), amount)
    donor, receiver = mixed[0:amount // 2 * 2:2], mixed[1:amount // 2 * 2:2]
    margin = jnp.minimum(lengths[donor] - 1, bound - lengths[receiver]) // 2
    margin = jnp.where((donor == order[0]) | (receiver == order[0]) | (lengths[receiver] == 0), 0, jnp.maximum(margin, 0))
    passed = jax.random.randint(jax.random.fold_in(own, 4), (amount // 2,), 0, 1 << 20) % (margin + 1)
    lengths = lengths.at[donor].add(-passed).at[receiver].add(passed)
    items = jnp.searchsorted(jnp.cumsum(lengths), jnp.arange(rows * top), side="right").astype(jnp.int32)
    listing = items.reshape(top, rows).T
    listing = listing[jax.random.permutation(jax.random.fold_in(own, 1), rows)]
    rotation = jax.random.randint(jax.random.fold_in(own, 2), (rows, 1), 0, top)
    return jnp.take_along_axis(listing, (jnp.arange(top)[None, :] + rotation) % top, axis=1)


def shares(count, total, reach, slope, full):
    loads = [(1 << 20) // math.isqrt(grade ** slope) + 1 for grade in range(1, count + 1)]
    largest = reach if full else min(reach, max(-(-total // count), total * loads[0] // sum(loads)))
    least = 1 if total - largest >= count - 1 else 0
    given, spare = [largest] + [least] * (count - 1), total - largest - least * (count - 1)
    while spare > 0:
        free = [i for i in range(1, count) if given[i] < largest] or [i for i in range(1, count) if given[i] < reach]
        mass, remaining = sum([loads[i] for i in free]), spare
        for i in free:
            extra = min(reach - given[i], max(1, remaining * loads[i] // mass), spare)
            given[i] = given[i] + extra
            spare = spare - extra
    return np.array(given)


def centred(rng, shape, spread, reach, shards=(), held_as=jnp.bfloat16):
    drawn = spread * jax.random.normal(rng, shape, jnp.float32)
    if shards:
        drawn = drawn * block_scale(rng, shape, shards, -0.22, 0.18)
    return jnp.clip(drawn, -reach, reach).astype(held_as)


def setup_inputs(seed: int = 0, part: int = 0) -> dict:
    key_list = jax.random.split(jax.random.key(seed), 9)
    own_keys = jax.random.split(jax.random.fold_in(key_list[8], part), 9)
    output_gradient = centred(own_keys[0], (TOKEN_ROWS, JOINED_WIDTH), 1.0, 6.0, ((0, 4), (1, 4)))
    normed_layer_input = centred(own_keys[1], (TOKEN_ROWS, MODEL_WIDTH), 0.05, 0.29882812, ((0, 4), (1, 4)))
    adapter_hidden = centred(own_keys[2], (TOKEN_ROWS, ADAPTER_RANK), 0.05, 0.29882812, ((0, 4),))
    query_key_value_weight = centred(key_list[3], (MODEL_WIDTH, JOINED_WIDTH), JOINED_WIDTH ** -0.5, 0.0625, ((0, 4), (1, 4)))
    adapter_down_factor = centred(own_keys[4], (ADAPTER_COUNT, ADAPTER_RANK, MODEL_WIDTH), (4 * ADAPTER_RANK) ** -0.5, 0.375, ((2, 4),))
    adapter_up_factor = centred(own_keys[5], (ADAPTER_COUNT, ADAPTER_RANK, JOINED_WIDTH), JOINED_WIDTH ** -0.5, 0.0625, ((2, 4),))
    block_adapter_table_keys = jax.random.split(jax.random.fold_in(own_keys[6], 1), BLOCK_COUNT // BPD)
    block_adapter_table_turns = jax.random.permutation(jax.random.fold_in(own_keys[6], 3), BLOCK_COUNT // BPD)
    block_adapter_table = jax.vmap(lambda own, number: shared_out(jax.random.fold_in(own_keys[6], 2), own, number, BPD, ADAPTER_COUNT, 1, CAP, 2))(block_adapter_table_keys, block_adapter_table_turns).reshape((BLOCK_COUNT, 1))
    block_live_rows = draw_block_live_rows(jax.random.fold_in(jax.random.fold_in(key_list[8], part), 71), part)
    return {"output_gradient": output_gradient, "normed_layer_input": normed_layer_input, "adapter_hidden": adapter_hidden, "query_key_value_weight": query_key_value_weight, "adapter_down_factor": adapter_down_factor, "adapter_up_factor": adapter_up_factor, "block_adapter_table": block_adapter_table, "block_live_rows": block_live_rows}


adapter_scale = 2.0


def reference(output_gradient, normed_layer_input, adapter_hidden, query_key_value_weight, adapter_down_factor, adapter_up_factor, block_adapter_table, block_live_rows):
    adapter_list = block_adapter_table[:, 0].astype(jnp.int32)
    offsets = jnp.arange(BLOCK_ROWS, dtype=jnp.int32)
    valid_row_mask = (offsets[None, :] < block_live_rows[:, None]).reshape(TOKEN_ROWS, 1)
    row_slot = jnp.repeat(adapter_list, BLOCK_ROWS).astype(jnp.int32)
    grad_blocks = output_gradient.reshape(BLOCK_COUNT, BLOCK_ROWS, JOINED_WIDTH)

    def project(packed):
        row_block, adapter_number = packed
        up_factor_rows = lax.dynamic_index_in_dim(adapter_up_factor, adapter_number, 0, keepdims=False)
        return lax.dot_general(row_block, up_factor_rows, (((1,), (1,)), ((), ())), preferred_element_type=jnp.float32)

    projected_rows = lax.map(project, (grad_blocks, adapter_list)).reshape(TOKEN_ROWS, ADAPTER_RANK)
    adapter_middle = jnp.where(valid_row_mask, projected_rows, jnp.zeros_like(projected_rows)).astype(jnp.bfloat16)

    col_width = JOINED_WIDTH // N_GY

    def column(running_sum, col_index):
        col_start = col_index * col_width
        grad_cols = lax.dynamic_slice_in_dim(output_gradient, col_start, col_width, 1)
        weight_cols = lax.dynamic_slice_in_dim(query_key_value_weight, col_start, col_width, 1)
        partial_sum = lax.dot_general(grad_cols, weight_cols, (((1,), (1,)), ((), ())), preferred_element_type=jnp.float32)
        rounded = lax.optimization_barrier(partial_sum.astype(jnp.bfloat16))
        return running_sum + rounded.astype(jnp.float32), None

    frozen_input_gradient, _ = lax.scan(column, jnp.zeros((TOKEN_ROWS, MODEL_WIDTH), jnp.float32), jnp.arange(N_GY, dtype=jnp.int32))

    def spread_rows(packed):
        row_block, adapter_number = packed
        down_factor_rows = lax.dynamic_index_in_dim(adapter_down_factor, adapter_number, 0, keepdims=False)
        return jnp.dot(row_block, down_factor_rows, preferred_element_type=jnp.float32)

    adapter_term = lax.map(spread_rows, (adapter_middle.reshape(BLOCK_COUNT, BLOCK_ROWS, ADAPTER_RANK), adapter_list)).reshape(TOKEN_ROWS, MODEL_WIDTH)
    input_gradient = (frozen_input_gradient + adapter_scale * adapter_term).astype(jnp.bfloat16)

    owning_mask = row_slot[:, None] == jnp.arange(ADAPTER_COUNT, dtype=jnp.int32)[None, :]
    hidden_valid_rows = jnp.where(valid_row_mask, adapter_hidden, jnp.zeros_like(adapter_hidden))
    hidden_spread = jnp.where(owning_mask[:, :, None], hidden_valid_rows[:, None, :], jnp.zeros_like(hidden_valid_rows)[:, None, :]).reshape(TOKEN_ROWS, ADAPTER_COUNT * ADAPTER_RANK)
    middle_spread = jnp.where(owning_mask[:, :, None], adapter_middle[:, None, :], jnp.zeros_like(adapter_middle)[:, None, :]).reshape(TOKEN_ROWS, ADAPTER_COUNT * ADAPTER_RANK)
    up_gradient = adapter_scale * lax.dot_general(hidden_spread, output_gradient, (((0,), (0,)), ((), ())), preferred_element_type=jnp.float32).reshape(ADAPTER_COUNT, ADAPTER_RANK, JOINED_WIDTH)
    down_gradient = adapter_scale * lax.dot_general(middle_spread, normed_layer_input, (((0,), (0,)), ((), ())), preferred_element_type=jnp.float32).reshape(ADAPTER_COUNT, ADAPTER_RANK, MODEL_WIDTH)
    return input_gradient, down_gradient, up_gradient
```

```python
import functools

import jax
import jax.numpy as jnp
from jax import lax
from jax.experimental import pallas as pl
from jax.experimental.pallas import tpu as pltpu
from jax.sharding import PartitionSpec as P

BLOCK_ROWS = 16
CHUNK = 64
ADAPTER_SCALE = 2.0
MESH = pl.DeviceIdType.MESH
F32 = jnp.float32
BF16 = jnp.bfloat16


def nt(a, b):
    return lax.dot_general(a, b, (((1,), (1,)), ((), ())), preferred_element_type=F32)


def tn(a, b):
    return lax.dot_general(a, b, (((0,), (0,)), ((), ())), preferred_element_type=F32)


def nn(a, b):
    return lax.dot_general(a, b, (((1,), (0,)), ((), ())), preferred_element_type=F32)


def tile_of(width, most):
    tile = most
    while width % tile:
        tile -= 128
    return tile


def kernel(
    n,
    dy_hbm, x_hbm, hid_ref, w_hbm, down_hbm, up_hbm, ads_ref, live_ref,
    out_ref, dgrad_ref, ugrad_ref,
    dy_all, w, x, down, up, part, part_in, adapter_term,
    hid_out, hid_in, proj_out, proj_in, mid, spread, dpart, dpart_in,
    load_sem, own_sem, z_send, z_recv, rs_send, rs_recv,
    hid_send, hid_recv, proj_send, proj_recv, mid_send, mid_recv, d_send, d_recv,
):
    z = lax.axis_index("gx")
    c_me = lax.axis_index("gy")
    tok, q = dy_hbm.shape
    width = w_hbm.shape[0]
    rank = hid_ref.shape[1]
    nc = tok // CHUNK
    tile_i = tile_of(width, 512)
    tile_q = tile_of(q, 640)

    def rows_of(b, c):
        return pl.ds(pl.multiple_of(b * tok + c * CHUNK, CHUNK), CHUNK)

    def chunk_rows(c):
        return pl.ds(pl.multiple_of(c * CHUNK, CHUNK), CHUNK)

    def own_copy(c):
        return pltpu.make_async_copy(
            dy_hbm.at[chunk_rows(c)], dy_all.at[rows_of(z, c)], own_sem.at[c]
        )

    def z_copy(direction, to, b, c):
        return pltpu.make_async_remote_copy(
            src_ref=dy_all.at[rows_of(b, c)],
            dst_ref=dy_all.at[rows_of(b, c)],
            send_sem=z_send.at[direction, b, c],
            recv_sem=z_recv.at[b, c],
            device_id={"gx": to},
            device_id_type=MESH,
        )

    def rs_copy(src, to, c):
        return pltpu.make_async_remote_copy(
            src_ref=part.at[rows_of(to, c)],
            dst_ref=part_in.at[src, chunk_rows(c)],
            send_sem=rs_send.at[to, c],
            recv_sem=rs_recv.at[src, c],
            device_id={"gy": to},
            device_id_type=MESH,
        )

    def hid_copy(src, to):
        return pltpu.make_async_remote_copy(
            src_ref=hid_out.at[to],
            dst_ref=hid_in.at[src],
            send_sem=hid_send.at[to],
            recv_sem=hid_recv.at[src],
            device_id={"gx": to},
            device_id_type=MESH,
        )

    def proj_copy(src, to):
        return pltpu.make_async_remote_copy(
            src_ref=proj_out,
            dst_ref=proj_in.at[src],
            send_sem=proj_send,
            recv_sem=proj_recv.at[src],
            device_id={"gy": to},
            device_id_type=MESH,
        )

    def mid_copy(to):
        return pltpu.make_async_remote_copy(
            src_ref=mid,
            dst_ref=mid,
            send_sem=mid_send.at[to],
            recv_sem=mid_recv,
            device_id={"gx": to},
            device_id_type=MESH,
        )

    def d_copy(src, to):
        return pltpu.make_async_remote_copy(
            src_ref=dpart.at[to],
            dst_ref=dpart_in.at[src],
            send_sem=d_send.at[to],
            recv_sem=d_recv.at[src],
            device_id={"gy": to},
            device_id_type=MESH,
        )

    loads = [
        pltpu.make_async_copy(up_hbm, up, load_sem.at[0]),
        pltpu.make_async_copy(w_hbm, w, load_sem.at[1]),
        pltpu.make_async_copy(x_hbm, x, load_sem.at[2]),
        pltpu.make_async_copy(down_hbm, down, load_sem.at[3]),
    ]
    for c in range(nc):
        own_copy(c).start()
    for copy in loads:
        copy.start()

    barrier = pltpu.get_barrier_semaphore()
    for step in range(1, n):
        pl.semaphore_signal(
            barrier, inc=1, device_id={"gx": lax.rem(z + step, n)}, device_id_type=MESH
        )
        pl.semaphore_signal(
            barrier, inc=1, device_id={"gy": lax.rem(c_me + step, n)}, device_id_type=MESH
        )
    pl.semaphore_wait(barrier, 2 * (n - 1))

    for c in range(nc):
        own_copy(c).wait()

        @pl.when(z > 0)
        def _():
            z_copy(1, z - 1, z, c).start()

        @pl.when(z < n - 1)
        def _():
            z_copy(0, z + 1, z, c).start()

    block_of = lax.broadcasted_iota(jnp.int32, (1, tok), 1) // BLOCK_ROWS
    offset = lax.broadcasted_iota(jnp.int32, (1, tok), 1) % BLOCK_ROWS
    ad_row = jnp.zeros((1, tok), jnp.int32)
    live_row = jnp.zeros((1, tok), jnp.int32)
    for b in range(tok // BLOCK_ROWS):
        ad_row = jnp.where(block_of == b, ads_ref[b, 0], ad_row)
        live_row = jnp.where(block_of == b, live_ref[b], live_row)
    is_live = offset < live_row

    loads[0].wait()
    own = dy_all[pl.ds(pl.multiple_of(z * tok, tok), tok), :]
    proj = jnp.zeros((rank, tok), F32)
    for s in range(n):
        proj = proj + jnp.where(ad_row == s, nt(up[s * rank:(s + 1) * rank, :], own), 0.0)
    proj_out[...] = proj.astype(BF16)

    @pl.when(c_me != z)
    def _():
        proj_copy(c_me, z).start()

    hid_t = jnp.transpose(hid_ref[...].astype(F32))
    for s in range(n):
        hid_out[s] = jnp.where((ad_row == s) & is_live, hid_t, 0.0).astype(BF16)

        @pl.when(z != s)
        def _():
            hid_copy(z, s).start()

    loads[1].wait()

    def spread_middle():
        @pl.when(c_me == z)
        def _():
            total = proj_out[...].astype(F32)
            for step in range(1, n):
                src = lax.rem(c_me + step, n)
                proj_copy(src, lax.rem(c_me + 1, n)).wait_recv()
                total = total + proj_in[src].astype(F32)
            mid[pl.ds(0, rank), :] = jnp.where(is_live, total, 0.0).astype(BF16)
            mid[pl.ds(rank, 16), :] = jnp.broadcast_to(ad_row.astype(F32), (16, tok)).astype(BF16)
            for step in range(1, n):
                mid_copy(lax.rem(z + step, n)).start()

    def adapter_work():
        @pl.when(c_me != z)
        def _():
            mid_copy(lax.rem(z + 1, n)).wait_recv()

        loads[2].wait()
        loads[3].wait()
        rows_ad = mid[rank:rank + 16, :].astype(F32)[0:1]
        values = mid[0:rank, :].astype(F32)
        for s in range(n):
            spread[s * rank:(s + 1) * rank, :] = jnp.where(rows_ad == float(s), values, 0.0).astype(BF16)

        def column(j, carry):
            cols = pl.ds(pl.multiple_of(j * tile_i, tile_i), tile_i)
            adapter_term[:, cols] = ADAPTER_SCALE * tn(spread[...], down[:, cols])
            grads = nn(spread[...], x[:, cols]).astype(BF16)
            for s in range(n):
                dpart[s, :, cols] = grads[s * rank:(s + 1) * rank]
            return carry

        lax.fori_loop(0, width // tile_i, column, 0)
        for step in range(1, n):
            d_copy(c_me, lax.rem(c_me + step, n)).start()

    def body(i, carry):
        @pl.when(i == 2 * nc)
        def _():
            spread_middle()

        @pl.when(i == 4 * nc)
        def _():
            adapter_work()

        d = i // (2 * nc)
        c = (i % (2 * nc)) // 2
        side = i % 2
        b = z + d * (2 * side - 1)

        @pl.when((b >= 0) & (b < n) & ((d > 0) | (side == 0)))
        def _():
            @pl.when(d > 0)
            def _():
                z_copy(side, lax.rem(z + 1, n), b, c).wait_recv()

                @pl.when((side == 0) & (z < n - 1))
                def _():
                    z_copy(0, z + 1, b, c).start()

                @pl.when((side == 1) & (z > 0))
                def _():
                    z_copy(1, z - 1, b, c).start()

            rows = rows_of(b, c)

            def column(j, carry):
                cols = pl.ds(pl.multiple_of(j * tile_i, tile_i), tile_i)
                part[rows, cols] = nt(dy_all[rows, :], w[cols, :]).astype(BF16)
                return carry

            lax.fori_loop(0, width // tile_i, column, 0)

            @pl.when(b != c_me)
            def _():
                rs_copy(c_me, b, c).start()

        return carry

    lax.fori_loop(0, 2 * nc * n, body, 0)

    for step in range(1, n):
        hid_copy(lax.rem(z + step, n), lax.rem(z + 1, n)).wait_recv()
    hid_in[z] = hid_out[z]

    def up_column(j, carry):
        cols = pl.ds(pl.multiple_of(j * tile_q, tile_q), tile_q)
        total = jnp.zeros((rank, tile_q), F32)
        for b in range(n):
            total = total + nn(hid_in[b], dy_all[b * tok:(b + 1) * tok, cols])
        ugrad_ref[:, cols] = ADAPTER_SCALE * total
        return carry

    lax.fori_loop(0, q // tile_q, up_column, 0)

    total = dpart[c_me].astype(F32)
    for step in range(1, n):
        src = lax.rem(c_me + step, n)
        d_copy(src, lax.rem(c_me + 1, n)).wait_recv()
        total = total + dpart_in[src].astype(F32)
    dgrad_ref[...] = ADAPTER_SCALE * total

    def finish(c, carry):
        rows = chunk_rows(c)
        total = adapter_term[rows, :] + part[rows_of(c_me, c), :].astype(F32)
        for step in range(1, n):
            src = lax.rem(c_me + step, n)
            rs_copy(src, lax.rem(c_me + 1, n), c).wait_recv()
            total = total + part_in[src, rows, :].astype(F32)
        out_ref[rows, :] = total.astype(BF16)
        return carry

    lax.fori_loop(0, nc, finish, 0)

    def drain(i, carry):
        b = i // nc
        c = i % nc

        @pl.when((b <= z) & (z < n - 1))
        def _():
            z_copy(0, z + 1, b, c).wait_send()

        @pl.when((b >= z) & (z > 0))
        def _():
            z_copy(1, z - 1, b, c).wait_send()

        @pl.when(b != c_me)
        def _():
            rs_copy(c_me, b, c).wait_send()

        return carry

    lax.fori_loop(0, n * nc, drain, 0)
    for step in range(1, n):
        hid_copy(z, lax.rem(z + step, n)).wait_send()
        d_copy(c_me, lax.rem(c_me + step, n)).wait_send()

        @pl.when(c_me == z)
        def _():
            mid_copy(lax.rem(z + step, n)).wait_send()

    @pl.when(c_me != z)
    def _():
        proj_copy(c_me, z).wait_send()


def per_device(n, dy, x, hidden, w, down, up, ads, live):
    tok, q = dy.shape
    width = w.shape[0]
    count, rank = down.shape[0], down.shape[1]
    nc = tok // CHUNK
    any_space = pl.BlockSpec(memory_space=pl.ANY)
    in_vmem = pl.BlockSpec(memory_space=pltpu.VMEM)
    in_smem = pl.BlockSpec(memory_space=pltpu.SMEM)
    dma = pltpu.SemaphoreType.DMA
    out, dgrad, ugrad = pl.pallas_call(
        functools.partial(kernel, n),
        out_shape=(
            jax.ShapeDtypeStruct((tok, width), BF16),
            jax.ShapeDtypeStruct((rank, width), F32),
            jax.ShapeDtypeStruct((rank, q), F32),
        ),
        in_specs=[any_space, any_space, in_vmem, any_space, any_space, any_space, in_smem, in_smem],
        out_specs=(in_vmem, in_vmem, in_vmem),
        scratch_shapes=[
            pltpu.VMEM((n * tok, q), BF16),
            pltpu.VMEM((width, q), BF16),
            pltpu.VMEM((tok, width), BF16),
            pltpu.VMEM((count * rank, width), BF16),
            pltpu.VMEM((count * rank, q), BF16),
            pltpu.VMEM((n * tok, width), BF16),
            pltpu.VMEM((n, tok, width), BF16),
            pltpu.VMEM((tok, width), F32),
            pltpu.VMEM((n, rank, tok), BF16),
            pltpu.VMEM((n, rank, tok), BF16),
            pltpu.VMEM((rank, tok), BF16),
            pltpu.VMEM((n, rank, tok), BF16),
            pltpu.VMEM((rank + 16, tok), BF16),
            pltpu.VMEM((count * rank, tok), BF16),
            pltpu.VMEM((n, rank, width), BF16),
            pltpu.VMEM((n, rank, width), BF16),
            dma((4,)),
            dma((nc,)),
            dma((2, n, nc)),
            dma((n, nc)),
            dma((n, nc)),
            dma((n, nc)),
            dma((n,)),
            dma((n,)),
            dma,
            dma((n,)),
            dma((n,)),
            dma,
            dma((n,)),
            dma((n,)),
        ],
        compiler_params=pltpu.CompilerParams(
            collective_id=0, has_side_effects=True, vmem_limit_bytes=56 * 1024 * 1024
        ),
        cost_estimate=pl.CostEstimate(
            flops=2 * n * tok * q * width, bytes_accessed=2 * width * q, transcendentals=0
        ),
    )(dy, x, hidden, w, down.reshape(count * rank, width), up.reshape(count * rank, q), ads, live)
    return out, dgrad[None], ugrad[None]


def solution(mesh):
    n = mesh.shape["gx"]
    assert mesh.shape["gy"] == n
    placed = (
        P(("grp", "gx"), "gy"),
        P(("grp", "gy"), "gx"),
        P(("grp", "gx"), None),
        P("gx", "gy"),
        P("grp", None, "gx"),
        P("grp", None, "gy"),
        P(("grp", "gx"), None),
        P(("grp", "gx")),
    )
    return jax.shard_map(
        functools.partial(per_device, n),
        mesh=mesh,
        in_specs=placed,
        out_specs=(
            P(("grp", "gy"), "gx"),
            P(("grp", "gy"), None, "gx"),
            P(("grp", "gx"), None, "gy"),
        ),
        check_vma=False,
    )
```

```python
import functools

import jax
import jax.numpy as jnp
from jax import lax
from jax.experimental import pallas as pl
from jax.experimental.pallas import tpu as pltpu
from jax.sharding import PartitionSpec as P

BLOCK_ROWS = 16
CHUNK = 64
ADAPTER_SCALE = 2.0
MESH = pl.DeviceIdType.MESH
F32 = jnp.float32
BF16 = jnp.bfloat16


def nt(a, b):
    return lax.dot_general(a, b, (((1,), (1,)), ((), ())), preferred_element_type=F32)


def tn(a, b):
    return lax.dot_general(a, b, (((0,), (0,)), ((), ())), preferred_element_type=F32)


def nn(a, b):
    return lax.dot_general(a, b, (((1,), (0,)), ((), ())), preferred_element_type=F32)


def tile_of(width, most):
    tile = most
    while width % tile:
        tile -= 128
    return tile


def kernel(
    n,
    dy_hbm, x_hbm, hid_ref, w_hbm, down_hbm, up_hbm, ads_ref, live_ref,
    out_hbm, dgrad_hbm, ugrad_hbm,
    dy_all, w, x, down, up, part, part_in, adapter_term,
    out_ref, dgrad_ref, ugrad_ref, hid_out, hid_in, proj_out, proj_in, mid, spread, dpart, dpart_in,
    load_sem, own_sem, z_send, z_recv, rs_send, rs_recv,
    hid_send, hid_recv, proj_send, proj_recv, mid_send, mid_recv, d_send, d_recv,
    hid2_send, hid2_recv, store_sem,
):
    z = lax.axis_index("gx")
    c_me = lax.axis_index("gy")
    tok, q = dy_hbm.shape
    width = w_hbm.shape[0]
    rank = hid_ref.shape[0]
    nc = tok // CHUNK
    parts = min(n, rank // 16)
    part_rank = rank // parts
    tile_i = tile_of(width, 512)
    nj = width // tile_i
    tile_q = tile_of(q, 640)

    def rows_of(b, c):
        return pl.ds(pl.multiple_of(b * tok + c * CHUNK, CHUNK), CHUNK)

    def chunk_rows(c):
        return pl.ds(pl.multiple_of(c * CHUNK, CHUNK), CHUNK)

    def own_copy(c):
        return pltpu.make_async_copy(
            dy_hbm.at[chunk_rows(c)], dy_all.at[rows_of(z, c)], own_sem.at[c]
        )

    def z_copy(direction, to, b, c):
        return pltpu.make_async_remote_copy(
            src_ref=dy_all.at[rows_of(b, c)],
            dst_ref=dy_all.at[rows_of(b, c)],
            send_sem=z_send.at[direction, b, c],
            recv_sem=z_recv.at[b, c],
            device_id={"gx": to},
            device_id_type=MESH,
        )

    def own_z_copy(direction, to, c):
        return pltpu.make_async_remote_copy(
            src_ref=dy_hbm.at[chunk_rows(c)],
            dst_ref=dy_all.at[rows_of(z, c)],
            send_sem=z_send.at[direction, z, c],
            recv_sem=z_recv.at[z, c],
            device_id={"gx": to},
            device_id_type=MESH,
        )

    def cols_of(j):
        return pl.ds(pl.multiple_of(j * tile_i, tile_i), tile_i)

    def rs_copy(src, to, c, j):
        return pltpu.make_async_remote_copy(
            src_ref=part.at[rows_of(to, c), cols_of(j)],
            dst_ref=part_in.at[src, chunk_rows(c), cols_of(j)],
            send_sem=rs_send.at[to, c, j],
            recv_sem=rs_recv.at[src, c, j],
            device_id={"gy": to},
            device_id_type=MESH,
        )

    def part_of(src):
        return pl.ds(pl.multiple_of(lax.min(src, parts - 1) * part_rank, part_rank), part_rank)

    my_part = part_of(c_me)

    def hid2_copy(src, to):
        return pltpu.make_async_remote_copy(
            src_ref=hid_in.at[:, part_of(src)],
            dst_ref=hid_in.at[:, part_of(src)],
            send_sem=hid2_send.at[to],
            recv_sem=hid2_recv.at[src],
            device_id={"gy": to},
            device_id_type=MESH,
        )

    def out_copy(c):
        return pltpu.make_async_copy(
            out_ref.at[chunk_rows(c)], out_hbm.at[chunk_rows(c)], store_sem.at[c]
        )

    dgrad_copy = pltpu.make_async_copy(dgrad_ref, dgrad_hbm, store_sem.at[nc])
    ugrad_copy = pltpu.make_async_copy(ugrad_ref, ugrad_hbm, store_sem.at[nc + 1])

    def hid_copy(src, to):
        return pltpu.make_async_remote_copy(
            src_ref=hid_out.at[to, my_part],
            dst_ref=hid_in.at[src, my_part],
            send_sem=hid_send.at[to],
            recv_sem=hid_recv.at[src],
            device_id={"gx": to},
            device_id_type=MESH,
        )

    def proj_copy(src, to):
        return pltpu.make_async_remote_copy(
            src_ref=proj_out,
            dst_ref=proj_in.at[src],
            send_sem=proj_send,
            recv_sem=proj_recv.at[src],
            device_id={"gy": to},
            device_id_type=MESH,
        )

    def mid_copy(to):
        return pltpu.make_async_remote_copy(
            src_ref=mid,
            dst_ref=mid,
            send_sem=mid_send.at[to],
            recv_sem=mid_recv,
            device_id={"gx": to},
            device_id_type=MESH,
        )

    def d_copy(src, to):
        return pltpu.make_async_remote_copy(
            src_ref=dpart.at[to],
            dst_ref=dpart_in.at[src],
            send_sem=d_send.at[to],
            recv_sem=d_recv.at[src],
            device_id={"gy": to},
            device_id_type=MESH,
        )

    loads = [
        pltpu.make_async_copy(up_hbm, up, load_sem.at[0]),
        pltpu.make_async_copy(w_hbm, w, load_sem.at[1]),
        pltpu.make_async_copy(x_hbm, x, load_sem.at[2]),
        pltpu.make_async_copy(down_hbm, down, load_sem.at[3]),
    ]
    for c in range(nc):
        own_copy(c).start()
    for copy in loads:
        copy.start()

    barrier = pltpu.get_barrier_semaphore()
    for step in range(1, n):
        pl.semaphore_signal(
            barrier, inc=1, device_id={"gx": lax.rem(z + step, n)}, device_id_type=MESH
        )
        pl.semaphore_signal(
            barrier, inc=1, device_id={"gy": lax.rem(c_me + step, n)}, device_id_type=MESH
        )
    pl.semaphore_wait(barrier, 2 * (n - 1))

    for c in range(nc):

        @pl.when(z > 0)
        def _():
            own_z_copy(1, z - 1, c).start()

        @pl.when(z < n - 1)
        def _():
            own_z_copy(0, z + 1, c).start()

    for c in range(nc):
        own_copy(c).wait()

    block_of = lax.broadcasted_iota(jnp.int32, (1, tok), 1) // BLOCK_ROWS
    offset = lax.broadcasted_iota(jnp.int32, (1, tok), 1) % BLOCK_ROWS
    ad_row = jnp.zeros((1, tok), jnp.int32)
    live_row = jnp.zeros((1, tok), jnp.int32)
    for b in range(tok // BLOCK_ROWS):
        ad_row = jnp.where(block_of == b, ads_ref[0, b], ad_row)
        live_row = jnp.where(block_of == b, live_ref[b], live_row)
    is_live = offset < live_row

    loads[0].wait()
    own = dy_all[pl.ds(pl.multiple_of(z * tok, tok), tok), :]
    proj = jnp.zeros((rank, tok), F32)
    for s in range(n):
        proj = proj + jnp.where(ad_row == s, nt(up[s * rank:(s + 1) * rank, :], own), 0.0)
    proj_out[...] = proj.astype(BF16)

    @pl.when(c_me != z)
    def _():
        proj_copy(c_me, z).start()

    hid_t = hid_ref[...].astype(F32)
    for s in range(n):
        hid_out[s] = jnp.where((ad_row == s) & is_live, hid_t, 0.0).astype(BF16)

        @pl.when((z != s) & (c_me < parts))
        def _():
            hid_copy(z, s).start()

    @pl.when(c_me < parts)
    def _():
        hid_in[z, my_part, :] = hid_out[z, my_part, :]

    loads[1].wait()

    def spread_middle():
        @pl.when(c_me == z)
        def _():
            total = proj_out[...].astype(F32)
            for step in range(1, n):
                src = lax.rem(c_me + step, n)
                proj_copy(src, lax.rem(c_me + 1, n)).wait_recv()
                total = total + proj_in[src].astype(F32)
            mid[pl.ds(0, rank), :] = jnp.where(is_live, total, 0.0).astype(BF16)
            mid[pl.ds(rank, 16), :] = jnp.broadcast_to(ad_row.astype(F32), (16, tok)).astype(BF16)
            for step in range(1, n):
                mid_copy(lax.rem(z + step, n)).start()

    def adapter_work():
        @pl.when(c_me != z)
        def _():
            mid_copy(lax.rem(z + 1, n)).wait_recv()

        loads[2].wait()
        loads[3].wait()
        rows_ad = mid[rank:rank + 16, :].astype(F32)[0:1]
        values = mid[0:rank, :].astype(F32)
        for s in range(n):
            spread[s * rank:(s + 1) * rank, :] = jnp.where(rows_ad == float(s), values, 0.0).astype(BF16)

        def column(j, carry):
            cols = pl.ds(pl.multiple_of(j * tile_i, tile_i), tile_i)
            adapter_term[:, cols] = ADAPTER_SCALE * tn(spread[...], down[:, cols])
            grads = nn(spread[...], x[:, cols]).astype(BF16)
            for s in range(n):
                dpart[s, :, cols] = grads[s * rank:(s + 1) * rank]
            return carry

        lax.fori_loop(0, width // tile_i, column, 0)
        for step in range(1, n):
            d_copy(c_me, lax.rem(c_me + step, n)).start()

        @pl.when(c_me < parts)
        def _():
            for step in range(1, n):
                hid_copy(lax.rem(z + step, n), lax.rem(z + 1, n)).wait_recv()
            for step in range(1, n):
                hid2_copy(c_me, lax.rem(c_me + step, n)).start()

    def body(i, carry):
        @pl.when(i == 2 * nc)
        def _():
            spread_middle()

        @pl.when(i == 3 * nc)
        def _():
            adapter_work()

        d = i // (2 * nc)
        c = (i % (2 * nc)) // 2
        side = i % 2
        b = z + d * (2 * side - 1)

        @pl.when((b >= 0) & (b < n) & ((d > 0) | (side == 0)))
        def _():
            @pl.when(d > 0)
            def _():
                z_copy(side, lax.rem(z + 1, n), b, c).wait_recv()

                @pl.when((side == 0) & (z < n - 1))
                def _():
                    z_copy(0, z + 1, b, c).start()

                @pl.when((side == 1) & (z > 0))
                def _():
                    z_copy(1, z - 1, b, c).start()

            rows = rows_of(b, c)

            def column(j, carry):
                cols = cols_of(j)
                part[rows, cols] = jnp.transpose(nt(w[cols, :], dy_all[rows, :])).astype(BF16)

                @pl.when(b != c_me)
                def _():
                    rs_copy(c_me, b, c, j).start()

                return carry

            lax.fori_loop(0, nj, column, 0)

        return carry

    lax.fori_loop(0, 2 * nc * n, body, 0)

    total = dpart[c_me].astype(F32)
    for step in range(1, n):
        src = lax.rem(c_me + step, n)
        d_copy(src, lax.rem(c_me + 1, n)).wait_recv()
        total = total + dpart_in[src].astype(F32)
    dgrad_ref[...] = ADAPTER_SCALE * total
    dgrad_copy.start()

    for step in range(1, n):
        src = lax.rem(c_me + step, n)

        @pl.when(src < parts)
        def _():
            hid2_copy(src, lax.rem(c_me + 1, n)).wait_recv()

    def up_column(j, carry):
        cols = pl.ds(pl.multiple_of(j * tile_q, tile_q), tile_q)
        total = jnp.zeros((rank, tile_q), F32)
        for b in range(n):
            total = total + nn(hid_in[b], dy_all[b * tok:(b + 1) * tok, cols])
        ugrad_ref[:, cols] = ADAPTER_SCALE * total
        return carry

    lax.fori_loop(0, q // tile_q, up_column, 0)
    ugrad_copy.start()

    def finish(i, carry):
        c = i // nj
        j = i % nj
        rows = chunk_rows(c)
        cols = cols_of(j)
        total = adapter_term[rows, cols] + part[rows_of(c_me, c), cols].astype(F32)
        for step in range(1, n):
            src = lax.rem(c_me + step, n)
            rs_copy(src, lax.rem(c_me + 1, n), c, j).wait_recv()
            total = total + part_in[src, rows, cols].astype(F32)
        out_ref[rows, cols] = total.astype(BF16)

        @pl.when(j == nj - 1)
        def _():
            out_copy(c).start()

        return carry

    lax.fori_loop(0, nc * nj, finish, 0)

    def drain(i, carry):
        b = i // nc
        c = i % nc

        @pl.when((b <= z) & (z < n - 1))
        def _():
            z_copy(0, z + 1, b, c).wait_send()

        @pl.when((b >= z) & (z > 0))
        def _():
            z_copy(1, z - 1, b, c).wait_send()

        @pl.when(b != c_me)
        def _():
            for j in range(nj):
                rs_copy(c_me, b, c, j).wait_send()

        return carry

    lax.fori_loop(0, n * nc, drain, 0)
    for step in range(1, n):
        d_copy(c_me, lax.rem(c_me + step, n)).wait_send()

        @pl.when(c_me < parts)
        def _():
            hid_copy(z, lax.rem(z + step, n)).wait_send()
            hid2_copy(c_me, lax.rem(c_me + step, n)).wait_send()

        @pl.when(c_me == z)
        def _():
            mid_copy(lax.rem(z + step, n)).wait_send()

    @pl.when(c_me != z)
    def _():
        proj_copy(c_me, z).wait_send()

    for c in range(nc):
        out_copy(c).wait()
    dgrad_copy.wait()
    ugrad_copy.wait()


def hand_over(a_hbm, b_hbm, c_hbm, a_out, b_out, c_out, sem):
    copies = [
        pltpu.make_async_copy(a_hbm, a_out, sem.at[0]),
        pltpu.make_async_copy(b_hbm, b_out, sem.at[1]),
        pltpu.make_async_copy(c_hbm, c_out, sem.at[2]),
    ]
    for copy in copies:
        copy.start()
    for copy in copies:
        copy.wait()


def per_device(n, dy, x, hidden, w, down, up, ads, live):
    tok, q = dy.shape
    width = w.shape[0]
    count, rank = down.shape[0], down.shape[1]
    nc = tok // CHUNK
    any_space = pl.BlockSpec(memory_space=pl.ANY)
    in_vmem = pl.BlockSpec(memory_space=pltpu.VMEM)
    in_smem = pl.BlockSpec(memory_space=pltpu.SMEM)
    dma = pltpu.SemaphoreType.DMA
    nj = width // tile_of(width, 512)
    shapes = (
        jax.ShapeDtypeStruct((tok, width), BF16),
        jax.ShapeDtypeStruct((rank, width), F32),
        jax.ShapeDtypeStruct((rank, q), F32),
    )
    results = pl.pallas_call(
        functools.partial(kernel, n),
        out_shape=shapes,
        in_specs=[any_space, any_space, in_vmem, any_space, any_space, any_space, in_smem, in_smem],
        out_specs=(any_space, any_space, any_space),
        scratch_shapes=[
            pltpu.VMEM((n * tok, q), BF16),
            pltpu.VMEM((width, q), BF16),
            pltpu.VMEM((tok, width), BF16),
            pltpu.VMEM((count * rank, width), BF16),
            pltpu.VMEM((count * rank, q), BF16),
            pltpu.VMEM((n * tok, width), BF16),
            pltpu.VMEM((n, tok, width), BF16),
            pltpu.VMEM((tok, width), F32),
            pltpu.VMEM((tok, width), BF16),
            pltpu.VMEM((rank, width), F32),
            pltpu.VMEM((rank, q), F32),
            pltpu.VMEM((n, rank, tok), BF16),
            pltpu.VMEM((n, rank, tok), BF16),
            pltpu.VMEM((rank, tok), BF16),
            pltpu.VMEM((n, rank, tok), BF16),
            pltpu.VMEM((rank + 16, tok), BF16),
            pltpu.VMEM((count * rank, tok), BF16),
            pltpu.VMEM((n, rank, width), BF16),
            pltpu.VMEM((n, rank, width), BF16),
            dma((4,)),
            dma((nc,)),
            dma((2, n, nc)),
            dma((n, nc)),
            dma((n, nc, nj)),
            dma((n, nc, nj)),
            dma((n,)),
            dma((n,)),
            dma,
            dma((n,)),
            dma((n,)),
            dma,
            dma((n,)),
            dma((n,)),
            dma((n,)),
            dma((n,)),
            dma((nc + 2,)),
        ],
        compiler_params=pltpu.CompilerParams(
            collective_id=0, has_side_effects=True, vmem_limit_bytes=56 * 1024 * 1024
        ),
        cost_estimate=pl.CostEstimate(
            flops=2 * n * tok * q * width, bytes_accessed=2 * width * q, transcendentals=0
        ),
    )(dy, x, hidden.T, w, down.reshape(count * rank, width), up.reshape(count * rank, q), ads.T, live)
    out, dgrad, ugrad = pl.pallas_call(
        hand_over,
        out_shape=shapes,
        in_specs=[any_space] * 3,
        out_specs=(any_space,) * 3,
        scratch_shapes=[dma((3,))],
    )(*results)
    return out, dgrad[None], ugrad[None]


def solution(mesh):
    n = mesh.shape["gx"]
    assert mesh.shape["gy"] == n
    placed = (
        P(("grp", "gx"), "gy"),
        P(("grp", "gy"), "gx"),
        P(("grp", "gx"), None),
        P("gx", "gy"),
        P("grp", None, "gx"),
        P("grp", None, "gy"),
        P(("grp", "gx"), None),
        P(("grp", "gx")),
    )
    return jax.shard_map(
        functools.partial(per_device, n),
        mesh=mesh,
        in_specs=placed,
        out_specs=(
            P(("grp", "gy"), "gx"),
            P(("grp", "gy"), None, "gx"),
            P(("grp", "gx"), None, "gy"),
        ),
        check_vma=False,
    )
```

```python
import functools

import jax
import jax.numpy as jnp
from jax import lax
from jax.experimental import pallas as pl
from jax.experimental.pallas import tpu as pltpu
from jax.sharding import PartitionSpec as P

BLOCK_ROWS = 16
CHUNK = 64
ADAPTER_SCALE = 2.0
MESH = pl.DeviceIdType.MESH
F32 = jnp.float32
BF16 = jnp.bfloat16


def nt(a, b):
    return lax.dot_general(a, b, (((1,), (1,)), ((), ())), preferred_element_type=F32)


def tn(a, b):
    return lax.dot_general(a, b, (((0,), (0,)), ((), ())), preferred_element_type=F32)


def nn(a, b):
    return lax.dot_general(a, b, (((1,), (0,)), ((), ())), preferred_element_type=F32)


def tile_of(width, most):
    tile = most
    while width % tile:
        tile -= 128
    return tile


def kernel(
    n,
    dy_hbm, x_hbm, hid_ref, w_hbm, down_hbm, up_hbm, ads_ref, live_ref,
    out_hbm, dgrad_hbm, ugrad_hbm,
    dy_all, w, x, down, up, part, part_in, adapter_term,
    out_ref, dgrad_ref, ugrad_ref, hid_out, hid_in, proj_out, proj_in, mid, spread, dpart, dpart_in,
    load_sem, own_sem, z_send, z_recv, rs_send, rs_recv,
    hid_send, hid_recv, proj_send, proj_recv, mid_send, mid_recv, d_send, d_recv,
    hid2_send, hid2_recv, store_sem,
):
    z = lax.axis_index("gx")
    c_me = lax.axis_index("gy")
    tok, q = dy_hbm.shape
    width = w_hbm.shape[0]
    rank = hid_ref.shape[0]
    nc = tok // CHUNK
    parts = min(n, rank // 16)
    part_rank = rank // parts
    tile_i = tile_of(width, 512)
    nj = width // tile_i
    tile_q = tile_of(q, 640)

    def rows_of(b, c):
        return pl.ds(pl.multiple_of(b * tok + c * CHUNK, CHUNK), CHUNK)

    def chunk_rows(c):
        return pl.ds(pl.multiple_of(c * CHUNK, CHUNK), CHUNK)

    def own_copy(c):
        return pltpu.make_async_copy(
            dy_hbm.at[chunk_rows(c)], dy_all.at[rows_of(z, c)], own_sem.at[c]
        )

    def z_copy(direction, to, b, c):
        return pltpu.make_async_remote_copy(
            src_ref=dy_all.at[rows_of(b, c)],
            dst_ref=dy_all.at[rows_of(b, c)],
            send_sem=z_send.at[direction, b, c],
            recv_sem=z_recv.at[b, c],
            device_id={"gx": to},
            device_id_type=MESH,
        )

    def own_z_copy(direction, to, c):
        return pltpu.make_async_remote_copy(
            src_ref=dy_hbm.at[chunk_rows(c)],
            dst_ref=dy_all.at[rows_of(z, c)],
            send_sem=z_send.at[direction, z, c],
            recv_sem=z_recv.at[z, c],
            device_id={"gx": to},
            device_id_type=MESH,
        )

    def cols_of(j):
        return pl.ds(pl.multiple_of(j * tile_i, tile_i), tile_i)

    def rs_copy(src, to, c, j):
        return pltpu.make_async_remote_copy(
            src_ref=part.at[rows_of(to, c), cols_of(j)],
            dst_ref=part_in.at[src, chunk_rows(c), cols_of(j)],
            send_sem=rs_send.at[to, c, j],
            recv_sem=rs_recv.at[src, c, j],
            device_id={"gy": to},
            device_id_type=MESH,
        )

    def part_of(src):
        return pl.ds(pl.multiple_of(lax.min(src, parts - 1) * part_rank, part_rank), part_rank)

    my_part = part_of(c_me)

    def hid2_copy(src, to):
        return pltpu.make_async_remote_copy(
            src_ref=hid_in.at[:, part_of(src)],
            dst_ref=hid_in.at[:, part_of(src)],
            send_sem=hid2_send.at[to],
            recv_sem=hid2_recv.at[src],
            device_id={"gy": to},
            device_id_type=MESH,
        )

    def out_copy(c):
        return pltpu.make_async_copy(
            out_ref.at[chunk_rows(c)], out_hbm.at[chunk_rows(c)], store_sem.at[c]
        )

    dgrad_copy = pltpu.make_async_copy(dgrad_ref, dgrad_hbm, store_sem.at[nc])
    ugrad_copy = pltpu.make_async_copy(ugrad_ref, ugrad_hbm, store_sem.at[nc + 1])

    def hid_copy(src, to):
        return pltpu.make_async_remote_copy(
            src_ref=hid_out.at[to, my_part],
            dst_ref=hid_in.at[src, my_part],
            send_sem=hid_send.at[to],
            recv_sem=hid_recv.at[src],
            device_id={"gx": to},
            device_id_type=MESH,
        )

    def proj_copy(src, to):
        return pltpu.make_async_remote_copy(
            src_ref=proj_out,
            dst_ref=proj_in.at[src],
            send_sem=proj_send,
            recv_sem=proj_recv.at[src],
            device_id={"gy": to},
            device_id_type=MESH,
        )

    def mid_copy(to):
        return pltpu.make_async_remote_copy(
            src_ref=mid,
            dst_ref=mid,
            send_sem=mid_send.at[to],
            recv_sem=mid_recv,
            device_id={"gx": to},
            device_id_type=MESH,
        )

    def d_copy(src, to):
        return pltpu.make_async_remote_copy(
            src_ref=dpart.at[to],
            dst_ref=dpart_in.at[src],
            send_sem=d_send.at[to],
            recv_sem=d_recv.at[src],
            device_id={"gy": to},
            device_id_type=MESH,
        )

    loads = [
        pltpu.make_async_copy(up_hbm, up, load_sem.at[0]),
        pltpu.make_async_copy(w_hbm, w, load_sem.at[1]),
        pltpu.make_async_copy(x_hbm, x, load_sem.at[2]),
        pltpu.make_async_copy(down_hbm, down, load_sem.at[3]),
    ]
    for c in range(nc):
        own_copy(c).start()
    for copy in loads:
        copy.start()

    barrier = pltpu.get_barrier_semaphore()
    for step in range(1, n):
        pl.semaphore_signal(
            barrier, inc=1, device_id={"gx": lax.rem(z + step, n)}, device_id_type=MESH
        )
        pl.semaphore_signal(
            barrier, inc=1, device_id={"gy": lax.rem(c_me + step, n)}, device_id_type=MESH
        )
    pl.semaphore_wait(barrier, 2 * (n - 1))

    for c in range(nc):

        @pl.when(z > 0)
        def _():
            own_z_copy(1, z - 1, c).start()

        @pl.when(z < n - 1)
        def _():
            own_z_copy(0, z + 1, c).start()

    for c in range(nc):
        own_copy(c).wait()

    block_of = lax.broadcasted_iota(jnp.int32, (1, tok), 1) // BLOCK_ROWS
    offset = lax.broadcasted_iota(jnp.int32, (1, tok), 1) % BLOCK_ROWS
    ad_row = jnp.zeros((1, tok), jnp.int32)
    live_row = jnp.zeros((1, tok), jnp.int32)
    for b in range(tok // BLOCK_ROWS):
        ad_row = jnp.where(block_of == b, ads_ref[0, b], ad_row)
        live_row = jnp.where(block_of == b, live_ref[b], live_row)
    is_live = offset < live_row

    loads[0].wait()
    own = dy_all[pl.ds(pl.multiple_of(z * tok, tok), tok), :]
    proj = jnp.zeros((rank, tok), F32)
    for s in range(n):
        proj = proj + jnp.where(ad_row == s, nt(up[s * rank:(s + 1) * rank, :], own), 0.0)
    proj_out[...] = proj.astype(BF16)

    @pl.when(c_me != z)
    def _():
        proj_copy(c_me, z).start()

    hid_t = hid_ref[...].astype(F32)
    for s in range(n):
        hid_out[s] = jnp.where((ad_row == s) & is_live, hid_t, 0.0).astype(BF16)

        @pl.when((z != s) & (c_me < parts))
        def _():
            hid_copy(z, s).start()

    @pl.when(c_me < parts)
    def _():
        hid_in[z, my_part, :] = hid_out[z, my_part, :]

    loads[1].wait()

    def spread_middle():
        @pl.when(c_me == z)
        def _():
            total = proj_out[...].astype(F32)
            for step in range(1, n):
                src = lax.rem(c_me + step, n)
                proj_copy(src, lax.rem(c_me + 1, n)).wait_recv()
                total = total + proj_in[src].astype(F32)
            mid[pl.ds(0, rank), :] = jnp.where(is_live, total, 0.0).astype(BF16)
            mid[pl.ds(rank, 16), :] = jnp.broadcast_to(ad_row.astype(F32), (16, tok)).astype(BF16)
            for step in range(1, n):
                mid_copy(lax.rem(z + step, n)).start()

    def adapter_work():
        @pl.when(c_me != z)
        def _():
            mid_copy(lax.rem(z + 1, n)).wait_recv()

        loads[2].wait()
        loads[3].wait()
        rows_ad = mid[rank:rank + 16, :].astype(F32)[0:1]
        values = mid[0:rank, :].astype(F32)
        for s in range(n):
            spread[s * rank:(s + 1) * rank, :] = jnp.where(rows_ad == float(s), values, 0.0).astype(BF16)

        def column(j, carry):
            cols = pl.ds(pl.multiple_of(j * tile_i, tile_i), tile_i)
            adapter_term[:, cols] = ADAPTER_SCALE * tn(spread[...], down[:, cols])
            grads = nn(spread[...], x[:, cols]).astype(BF16)
            for s in range(n):
                dpart[s, :, cols] = grads[s * rank:(s + 1) * rank]
            return carry

        lax.fori_loop(0, width // tile_i, column, 0)
        for step in range(1, n):
            d_copy(c_me, lax.rem(c_me + step, n)).start()

        @pl.when(c_me < parts)
        def _():
            for step in range(1, n):
                hid_copy(lax.rem(z + step, n), lax.rem(z + 1, n)).wait_recv()
            for step in range(1, n):
                hid2_copy(c_me, lax.rem(c_me + step, n)).start()

    def body(i, carry):
        @pl.when(i == 2 * nc)
        def _():
            spread_middle()

        @pl.when(i == 3 * nc)
        def _():
            adapter_work()

        d = i // (2 * nc)
        c = (i % (2 * nc)) // 2
        side = i % 2
        b = z + d * (2 * side - 1)

        @pl.when((b >= 0) & (b < n) & ((d > 0) | (side == 0)))
        def _():
            @pl.when(d > 0)
            def _():
                z_copy(side, lax.rem(z + 1, n), b, c).wait_recv()

                @pl.when((side == 0) & (z < n - 1))
                def _():
                    z_copy(0, z + 1, b, c).start()

                @pl.when((side == 1) & (z > 0))
                def _():
                    z_copy(1, z - 1, b, c).start()

            rows = rows_of(b, c)

            def column(j, carry):
                cols = cols_of(j)
                part[rows, cols] = jnp.transpose(nt(w[cols, :], dy_all[rows, :])).astype(BF16)

                @pl.when(b != c_me)
                def _():
                    rs_copy(c_me, b, c, j).start()

                return carry

            lax.fori_loop(0, nj, column, 0)

        return carry

    lax.fori_loop(0, 2 * nc * n, body, 0)

    total = dpart[c_me].astype(F32)
    for step in range(1, n):
        src = lax.rem(c_me + step, n)
        d_copy(src, lax.rem(c_me + 1, n)).wait_recv()
        total = total + dpart_in[src].astype(F32)
    dgrad_ref[...] = ADAPTER_SCALE * total
    dgrad_copy.start()

    for step in range(1, n):
        src = lax.rem(c_me + step, n)

        @pl.when(src < parts)
        def _():
            hid2_copy(src, lax.rem(c_me + 1, n)).wait_recv()

    def up_column(j, carry):
        cols = pl.ds(pl.multiple_of(j * tile_q, tile_q), tile_q)
        total = jnp.zeros((rank, tile_q), F32)
        for b in range(n):
            total = total + nn(hid_in[b], dy_all[b * tok:(b + 1) * tok, cols])
        ugrad_ref[:, cols] = ADAPTER_SCALE * total
        return carry

    lax.fori_loop(0, q // tile_q, up_column, 0)
    ugrad_copy.start()

    def finish(i, carry):
        c = i // nj
        j = i % nj
        rows = chunk_rows(c)
        cols = cols_of(j)
        total = adapter_term[rows, cols] + part[rows_of(c_me, c), cols].astype(F32)
        for step in range(1, n):
            src = lax.rem(c_me + step, n)
            rs_copy(src, lax.rem(c_me + 1, n), c, j).wait_recv()
            total = total + part_in[src, rows, cols].astype(F32)
        out_ref[rows, cols] = total.astype(BF16)

        @pl.when(j == nj - 1)
        def _():
            out_copy(c).start()

        return carry

    lax.fori_loop(0, nc * nj, finish, 0)

    def drain(i, carry):
        b = i // nc
        c = i % nc

        @pl.when((b <= z) & (z < n - 1))
        def _():
            z_copy(0, z + 1, b, c).wait_send()

        @pl.when((b >= z) & (z > 0))
        def _():
            z_copy(1, z - 1, b, c).wait_send()

        @pl.when(b != c_me)
        def _():
            for j in range(nj):
                rs_copy(c_me, b, c, j).wait_send()

        return carry

    lax.fori_loop(0, n * nc, drain, 0)
    for step in range(1, n):
        d_copy(c_me, lax.rem(c_me + step, n)).wait_send()

        @pl.when(c_me < parts)
        def _():
            hid_copy(z, lax.rem(z + step, n)).wait_send()
            hid2_copy(c_me, lax.rem(c_me + step, n)).wait_send()

        @pl.when(c_me == z)
        def _():
            mid_copy(lax.rem(z + step, n)).wait_send()

    @pl.when(c_me != z)
    def _():
        proj_copy(c_me, z).wait_send()

    for c in range(nc):
        out_copy(c).wait()
    dgrad_copy.wait()
    ugrad_copy.wait()


def hand_over(a_hbm, b_hbm, c_hbm, a_out, b_out, c_out, a, b, c, in_sem, out_sem):
    pieces = []
    for source, held, target in ((a_hbm, a, a_out), (b_hbm, b, b_out), (c_hbm, c, c_out)):
        half = source.shape[0] // 2
        for start in (0, half):
            pieces.append((source.at[start:start + half], held.at[start:start + half], target.at[start:start + half]))
    arrive = [pltpu.make_async_copy(p[0], p[1], in_sem.at[k]) for k, p in enumerate(pieces)]
    leave = [pltpu.make_async_copy(p[1], p[2], out_sem.at[k]) for k, p in enumerate(pieces)]
    for copy in arrive:
        copy.start()
    for k in range(len(pieces)):
        arrive[k].wait()
        leave[k].start()
    for copy in leave:
        copy.wait()


def per_device(n, dy, x, hidden, w, down, up, ads, live):
    tok, q = dy.shape
    width = w.shape[0]
    count, rank = down.shape[0], down.shape[1]
    nc = tok // CHUNK
    any_space = pl.BlockSpec(memory_space=pl.ANY)
    in_vmem = pl.BlockSpec(memory_space=pltpu.VMEM)
    in_smem = pl.BlockSpec(memory_space=pltpu.SMEM)
    dma = pltpu.SemaphoreType.DMA
    nj = width // tile_of(width, 512)
    shapes = (
        jax.ShapeDtypeStruct((tok, width), BF16),
        jax.ShapeDtypeStruct((rank, width), F32),
        jax.ShapeDtypeStruct((rank, q), F32),
    )
    results = pl.pallas_call(
        functools.partial(kernel, n),
        out_shape=shapes,
        in_specs=[any_space, any_space, in_vmem, any_space, any_space, any_space, in_smem, in_smem],
        out_specs=(any_space, any_space, any_space),
        scratch_shapes=[
            pltpu.VMEM((n * tok, q), BF16),
            pltpu.VMEM((width, q), BF16),
            pltpu.VMEM((tok, width), BF16),
            pltpu.VMEM((count * rank, width), BF16),
            pltpu.VMEM((count * rank, q), BF16),
            pltpu.VMEM((n * tok, width), BF16),
            pltpu.VMEM((n, tok, width), BF16),
            pltpu.VMEM((tok, width), F32),
            pltpu.VMEM((tok, width), BF16),
            pltpu.VMEM((rank, width), F32),
            pltpu.VMEM((rank, q), F32),
            pltpu.VMEM((n, rank, tok), BF16),
            pltpu.VMEM((n, rank, tok), BF16),
            pltpu.VMEM((rank, tok), BF16),
            pltpu.VMEM((n, rank, tok), BF16),
            pltpu.VMEM((rank + 16, tok), BF16),
            pltpu.VMEM((count * rank, tok), BF16),
            pltpu.VMEM((n, rank, width), BF16),
            pltpu.VMEM((n, rank, width), BF16),
            dma((4,)),
            dma((nc,)),
            dma((2, n, nc)),
            dma((n, nc)),
            dma((n, nc, nj)),
            dma((n, nc, nj)),
            dma((n,)),
            dma((n,)),
            dma,
            dma((n,)),
            dma((n,)),
            dma,
            dma((n,)),
            dma((n,)),
            dma((n,)),
            dma((n,)),
            dma((nc + 2,)),
        ],
        compiler_params=pltpu.CompilerParams(
            collective_id=0, has_side_effects=True, vmem_limit_bytes=56 * 1024 * 1024
        ),
        cost_estimate=pl.CostEstimate(
            flops=2 * n * tok * q * width, bytes_accessed=2 * width * q, transcendentals=0
        ),
    )(dy, x, hidden.T, w, down.reshape(count * rank, width), up.reshape(count * rank, q), ads.T, live)
    out, dgrad, ugrad = pl.pallas_call(
        hand_over,
        out_shape=shapes,
        in_specs=[any_space] * 3,
        out_specs=(any_space,) * 3,
        scratch_shapes=[pltpu.VMEM(t.shape, t.dtype) for t in shapes] + [dma((6,)), dma((6,))],
    )(*results)
    return out, dgrad[None], ugrad[None]


def solution(mesh):
    n = mesh.shape["gx"]
    assert mesh.shape["gy"] == n
    placed = (
        P(("grp", "gx"), "gy"),
        P(("grp", "gy"), "gx"),
        P(("grp", "gx"), None),
        P("gx", "gy"),
        P("grp", None, "gx"),
        P("grp", None, "gy"),
        P(("grp", "gx"), None),
        P(("grp", "gx")),
    )
    return jax.shard_map(
        functools.partial(per_device, n),
        mesh=mesh,
        in_specs=placed,
        out_specs=(
            P(("grp", "gy"), "gx"),
            P(("grp", "gy"), None, "gx"),
            P(("grp", "gx"), None, "gy"),
        ),
        check_vma=False,
    )
```

```python
import functools

import jax
import jax.numpy as jnp
from jax import lax
from jax.experimental import pallas as pl
from jax.experimental.pallas import tpu as pltpu
from jax.sharding import PartitionSpec as P

BLOCK_ROWS = 16
CHUNK = 64
ADAPTER_SCALE = 2.0
MESH = pl.DeviceIdType.MESH
F32 = jnp.float32
BF16 = jnp.bfloat16


def nt(a, b):
    return lax.dot_general(a, b, (((1,), (1,)), ((), ())), preferred_element_type=F32)


def tn(a, b):
    return lax.dot_general(a, b, (((0,), (0,)), ((), ())), preferred_element_type=F32)


def nn(a, b):
    return lax.dot_general(a, b, (((1,), (0,)), ((), ())), preferred_element_type=F32)


def tile_of(width, most):
    tile = most
    while width % tile:
        tile -= 128
    return tile


def kernel(
    n,
    dy_hbm, x_hbm, hid_ref, w_hbm, down_hbm, up_hbm, ads_ref, live_ref,
    out_hbm, dgrad_hbm, ugrad_hbm,
    dy_all, w, x, down, up, part, part_in, adapter_term,
    out_ref, dgrad_ref, ugrad_ref, hid_out, hid_in, proj_out, proj_in, mid, spread, dpart, dpart_in,
    load_sem, own_sem, z_send, z_recv, rs_send, rs_recv,
    hid_send, hid_recv, proj_send, proj_recv, mid_send, mid_recv, d_send, d_recv,
    hid2_send, hid2_recv, store_sem,
):
    z = lax.axis_index("gx")
    c_me = lax.axis_index("gy")
    tok, q = dy_hbm.shape
    width = w_hbm.shape[0]
    rank = hid_ref.shape[0]
    nc = tok // CHUNK
    parts = min(n, rank // 16)
    part_rank = rank // parts
    tile_i = tile_of(width, 256)
    nj = width // tile_i
    tile_q = tile_of(q, 640)

    def rows_of(b, c):
        return pl.ds(pl.multiple_of(b * tok + c * CHUNK, CHUNK), CHUNK)

    def chunk_rows(c):
        return pl.ds(pl.multiple_of(c * CHUNK, CHUNK), CHUNK)

    def own_copy(c):
        return pltpu.make_async_copy(
            dy_hbm.at[chunk_rows(c)], dy_all.at[rows_of(z, c)], own_sem.at[c]
        )

    def z_copy(direction, to, b, c):
        return pltpu.make_async_remote_copy(
            src_ref=dy_all.at[rows_of(b, c)],
            dst_ref=dy_all.at[rows_of(b, c)],
            send_sem=z_send.at[direction, b, c],
            recv_sem=z_recv.at[b, c],
            device_id={"gx": to},
            device_id_type=MESH,
        )

    def own_z_copy(direction, to, c):
        return pltpu.make_async_remote_copy(
            src_ref=dy_hbm.at[chunk_rows(c)],
            dst_ref=dy_all.at[rows_of(z, c)],
            send_sem=z_send.at[direction, z, c],
            recv_sem=z_recv.at[z, c],
            device_id={"gx": to},
            device_id_type=MESH,
        )

    def cols_of(j):
        return pl.ds(pl.multiple_of(j * tile_i, tile_i), tile_i)

    def rs_copy(src, to, c, j):
        return pltpu.make_async_remote_copy(
            src_ref=part.at[rows_of(to, c), cols_of(j)],
            dst_ref=part_in.at[src, chunk_rows(c), cols_of(j)],
            send_sem=rs_send.at[to, c, j],
            recv_sem=rs_recv.at[src, c, j],
            device_id={"gy": to},
            device_id_type=MESH,
        )

    def part_of(src):
        return pl.ds(pl.multiple_of(lax.min(src, parts - 1) * part_rank, part_rank), part_rank)

    my_part = part_of(c_me)

    def hid2_copy(src, to):
        return pltpu.make_async_remote_copy(
            src_ref=hid_in.at[:, part_of(src)],
            dst_ref=hid_in.at[:, part_of(src)],
            send_sem=hid2_send.at[to],
            recv_sem=hid2_recv.at[src],
            device_id={"gy": to},
            device_id_type=MESH,
        )

    def out_copy(c):
        return pltpu.make_async_copy(
            out_ref.at[chunk_rows(c)], out_hbm.at[chunk_rows(c)], store_sem.at[c]
        )

    dgrad_copy = pltpu.make_async_copy(dgrad_ref, dgrad_hbm, store_sem.at[nc])
    ugrad_copy = pltpu.make_async_copy(ugrad_ref, ugrad_hbm, store_sem.at[nc + 1])

    def hid_copy(src, to):
        return pltpu.make_async_remote_copy(
            src_ref=hid_out.at[to, my_part],
            dst_ref=hid_in.at[src, my_part],
            send_sem=hid_send.at[to],
            recv_sem=hid_recv.at[src],
            device_id={"gx": to},
            device_id_type=MESH,
        )

    def proj_copy(src, to):
        return pltpu.make_async_remote_copy(
            src_ref=proj_out,
            dst_ref=proj_in.at[src],
            send_sem=proj_send,
            recv_sem=proj_recv.at[src],
            device_id={"gy": to},
            device_id_type=MESH,
        )

    def mid_copy(to):
        return pltpu.make_async_remote_copy(
            src_ref=mid,
            dst_ref=mid,
            send_sem=mid_send.at[to],
            recv_sem=mid_recv,
            device_id={"gx": to},
            device_id_type=MESH,
        )

    def d_copy(src, to):
        return pltpu.make_async_remote_copy(
            src_ref=dpart.at[to],
            dst_ref=dpart_in.at[src],
            send_sem=d_send.at[to],
            recv_sem=d_recv.at[src],
            device_id={"gy": to},
            device_id_type=MESH,
        )

    loads = [
        pltpu.make_async_copy(up_hbm, up, load_sem.at[0]),
        pltpu.make_async_copy(w_hbm, w, load_sem.at[1]),
        pltpu.make_async_copy(x_hbm, x, load_sem.at[2]),
        pltpu.make_async_copy(down_hbm, down, load_sem.at[3]),
    ]
    for c in range(nc):
        own_copy(c).start()
    for copy in loads:
        copy.start()

    barrier = pltpu.get_barrier_semaphore()
    for step in range(1, n):
        pl.semaphore_signal(
            barrier, inc=1, device_id={"gx": lax.rem(z + step, n)}, device_id_type=MESH
        )
        pl.semaphore_signal(
            barrier, inc=1, device_id={"gy": lax.rem(c_me + step, n)}, device_id_type=MESH
        )
    pl.semaphore_wait(barrier, 2 * (n - 1))

    for c in range(nc):

        @pl.when(z > 0)
        def _():
            own_z_copy(1, z - 1, c).start()

        @pl.when(z < n - 1)
        def _():
            own_z_copy(0, z + 1, c).start()

    for c in range(nc):
        own_copy(c).wait()

    block_of = lax.broadcasted_iota(jnp.int32, (1, tok), 1) // BLOCK_ROWS
    offset = lax.broadcasted_iota(jnp.int32, (1, tok), 1) % BLOCK_ROWS
    ad_row = jnp.zeros((1, tok), jnp.int32)
    live_row = jnp.zeros((1, tok), jnp.int32)
    for b in range(tok // BLOCK_ROWS):
        ad_row = jnp.where(block_of == b, ads_ref[0, b], ad_row)
        live_row = jnp.where(block_of == b, live_ref[b], live_row)
    is_live = offset < live_row

    loads[0].wait()
    own = dy_all[pl.ds(pl.multiple_of(z * tok, tok), tok), :]
    proj = jnp.zeros((rank, tok), F32)
    for s in range(n):
        proj = proj + jnp.where(ad_row == s, nt(up[s * rank:(s + 1) * rank, :], own), 0.0)
    proj_out[...] = proj.astype(BF16)

    @pl.when(c_me != z)
    def _():
        proj_copy(c_me, z).start()

    hid_t = hid_ref[...].astype(F32)
    for s in range(n):
        hid_out[s] = jnp.where((ad_row == s) & is_live, hid_t, 0.0).astype(BF16)

        @pl.when((z != s) & (c_me < parts))
        def _():
            hid_copy(z, s).start()

    @pl.when(c_me < parts)
    def _():
        hid_in[z, my_part, :] = hid_out[z, my_part, :]

    loads[1].wait()

    def spread_middle():
        @pl.when(c_me == z)
        def _():
            total = proj_out[...].astype(F32)
            for step in range(1, n):
                src = lax.rem(c_me + step, n)
                proj_copy(src, lax.rem(c_me + 1, n)).wait_recv()
                total = total + proj_in[src].astype(F32)
            mid[pl.ds(0, rank), :] = jnp.where(is_live, total, 0.0).astype(BF16)
            mid[pl.ds(rank, 16), :] = jnp.broadcast_to(ad_row.astype(F32), (16, tok)).astype(BF16)
            for step in range(1, n):
                mid_copy(lax.rem(z + step, n)).start()

    def adapter_work():
        @pl.when(c_me != z)
        def _():
            mid_copy(lax.rem(z + 1, n)).wait_recv()

        loads[2].wait()
        loads[3].wait()
        rows_ad = mid[rank:rank + 16, :].astype(F32)[0:1]
        values = mid[0:rank, :].astype(F32)
        for s in range(n):
            spread[s * rank:(s + 1) * rank, :] = jnp.where(rows_ad == float(s), values, 0.0).astype(BF16)

        def column(j, carry):
            cols = pl.ds(pl.multiple_of(j * tile_i, tile_i), tile_i)
            adapter_term[:, cols] = ADAPTER_SCALE * tn(spread[...], down[:, cols])
            grads = nn(spread[...], x[:, cols]).astype(BF16)
            for s in range(n):
                dpart[s, :, cols] = grads[s * rank:(s + 1) * rank]
            return carry

        lax.fori_loop(0, width // tile_i, column, 0)
        for step in range(1, n):
            d_copy(c_me, lax.rem(c_me + step, n)).start()

        @pl.when(c_me < parts)
        def _():
            for step in range(1, n):
                hid_copy(lax.rem(z + step, n), lax.rem(z + 1, n)).wait_recv()
            for step in range(1, n):
                hid2_copy(c_me, lax.rem(c_me + step, n)).start()

    def body(i, carry):
        @pl.when(i == 2 * nc)
        def _():
            spread_middle()

        @pl.when(i == 3 * nc)
        def _():
            adapter_work()

        d = i // (2 * nc)
        c = (i % (2 * nc)) // 2
        side = i % 2
        b = z + d * (2 * side - 1)

        @pl.when((b >= 0) & (b < n) & ((d > 0) | (side == 0)))
        def _():
            @pl.when(d > 0)
            def _():
                z_copy(side, lax.rem(z + 1, n), b, c).wait_recv()

                @pl.when((side == 0) & (z < n - 1))
                def _():
                    z_copy(0, z + 1, b, c).start()

                @pl.when((side == 1) & (z > 0))
                def _():
                    z_copy(1, z - 1, b, c).start()

            rows = rows_of(b, c)

            def column(j, carry):
                cols = cols_of(j)
                part[rows, cols] = jnp.transpose(nt(w[cols, :], dy_all[rows, :])).astype(BF16)

                @pl.when(b != c_me)
                def _():
                    rs_copy(c_me, b, c, j).start()

                return carry

            lax.fori_loop(0, nj, column, 0)

        return carry

    lax.fori_loop(0, 2 * nc * n, body, 0)

    total = dpart[c_me].astype(F32)
    for step in range(1, n):
        src = lax.rem(c_me + step, n)
        d_copy(src, lax.rem(c_me + 1, n)).wait_recv()
        total = total + dpart_in[src].astype(F32)
    dgrad_ref[...] = ADAPTER_SCALE * total
    dgrad_copy.start()

    for step in range(1, n):
        src = lax.rem(c_me + step, n)

        @pl.when(src < parts)
        def _():
            hid2_copy(src, lax.rem(c_me + 1, n)).wait_recv()

    def up_column(j, carry):
        cols = pl.ds(pl.multiple_of(j * tile_q, tile_q), tile_q)
        total = jnp.zeros((rank, tile_q), F32)
        for b in range(n):
            total = total + nn(hid_in[b], dy_all[b * tok:(b + 1) * tok, cols])
        ugrad_ref[:, cols] = ADAPTER_SCALE * total
        return carry

    lax.fori_loop(0, q // tile_q, up_column, 0)
    ugrad_copy.start()

    def finish(i, carry):
        c = i // nj
        j = i % nj
        rows = chunk_rows(c)
        cols = cols_of(j)
        total = adapter_term[rows, cols] + part[rows_of(c_me, c), cols].astype(F32)
        for step in range(1, n):
            src = lax.rem(c_me + step, n)
            rs_copy(src, lax.rem(c_me + 1, n), c, j).wait_recv()
            total = total + part_in[src, rows, cols].astype(F32)
        out_ref[rows, cols] = total.astype(BF16)

        @pl.when(j == nj - 1)
        def _():
            out_copy(c).start()

        return carry

    lax.fori_loop(0, nc * nj, finish, 0)

    def drain(i, carry):
        b = i // nc
        c = i % nc

        @pl.when((b <= z) & (z < n - 1))
        def _():
            z_copy(0, z + 1, b, c).wait_send()

        @pl.when((b >= z) & (z > 0))
        def _():
            z_copy(1, z - 1, b, c).wait_send()

        @pl.when(b != c_me)
        def _():
            for j in range(nj):
                rs_copy(c_me, b, c, j).wait_send()

        return carry

    lax.fori_loop(0, n * nc, drain, 0)
    for step in range(1, n):
        d_copy(c_me, lax.rem(c_me + step, n)).wait_send()

        @pl.when(c_me < parts)
        def _():
            hid_copy(z, lax.rem(z + step, n)).wait_send()
            hid2_copy(c_me, lax.rem(c_me + step, n)).wait_send()

        @pl.when(c_me == z)
        def _():
            mid_copy(lax.rem(z + step, n)).wait_send()

    @pl.when(c_me != z)
    def _():
        proj_copy(c_me, z).wait_send()

    for c in range(nc):
        out_copy(c).wait()
    dgrad_copy.wait()
    ugrad_copy.wait()


def hand_over(a_hbm, b_hbm, c_hbm, a_out, b_out, c_out, a, b, c, in_sem, out_sem):
    pieces = []
    for source, held, target in ((a_hbm, a, a_out), (b_hbm, b, b_out), (c_hbm, c, c_out)):
        quarter = source.shape[0] // 4
        for start in range(0, source.shape[0], quarter):
            pieces.append((source.at[start:start + quarter], held.at[start:start + quarter], target.at[start:start + quarter]))
    arrive = [pltpu.make_async_copy(p[0], p[1], in_sem.at[k]) for k, p in enumerate(pieces)]
    leave = [pltpu.make_async_copy(p[1], p[2], out_sem.at[k]) for k, p in enumerate(pieces)]
    for copy in arrive:
        copy.start()
    for k in range(len(pieces)):
        arrive[k].wait()
        leave[k].start()
    for copy in leave:
        copy.wait()


def per_device(n, dy, x, hidden, w, down, up, ads, live):
    tok, q = dy.shape
    width = w.shape[0]
    count, rank = down.shape[0], down.shape[1]
    nc = tok // CHUNK
    any_space = pl.BlockSpec(memory_space=pl.ANY)
    in_vmem = pl.BlockSpec(memory_space=pltpu.VMEM)
    in_smem = pl.BlockSpec(memory_space=pltpu.SMEM)
    dma = pltpu.SemaphoreType.DMA
    nj = width // tile_of(width, 256)
    shapes = (
        jax.ShapeDtypeStruct((tok, width), BF16),
        jax.ShapeDtypeStruct((rank, width), F32),
        jax.ShapeDtypeStruct((rank, q), F32),
    )
    results = pl.pallas_call(
        functools.partial(kernel, n),
        out_shape=shapes,
        in_specs=[any_space, any_space, in_vmem, any_space, any_space, any_space, in_smem, in_smem],
        out_specs=(any_space, any_space, any_space),
        scratch_shapes=[
            pltpu.VMEM((n * tok, q), BF16),
            pltpu.VMEM((width, q), BF16),
            pltpu.VMEM((tok, width), BF16),
            pltpu.VMEM((count * rank, width), BF16),
            pltpu.VMEM((count * rank, q), BF16),
            pltpu.VMEM((n * tok, width), BF16),
            pltpu.VMEM((n, tok, width), BF16),
            pltpu.VMEM((tok, width), F32),
            pltpu.VMEM((tok, width), BF16),
            pltpu.VMEM((rank, width), F32),
            pltpu.VMEM((rank, q), F32),
            pltpu.VMEM((n, rank, tok), BF16),
            pltpu.VMEM((n, rank, tok), BF16),
            pltpu.VMEM((rank, tok), BF16),
            pltpu.VMEM((n, rank, tok), BF16),
            pltpu.VMEM((rank + 16, tok), BF16),
            pltpu.VMEM((count * rank, tok), BF16),
            pltpu.VMEM((n, rank, width), BF16),
            pltpu.VMEM((n, rank, width), BF16),
            dma((4,)),
            dma((nc,)),
            dma((2, n, nc)),
            dma((n, nc)),
            dma((n, nc, nj)),
            dma((n, nc, nj)),
            dma((n,)),
            dma((n,)),
            dma,
            dma((n,)),
            dma((n,)),
            dma,
            dma((n,)),
            dma((n,)),
            dma((n,)),
            dma((n,)),
            dma((nc + 2,)),
        ],
        compiler_params=pltpu.CompilerParams(
            collective_id=0, has_side_effects=True, vmem_limit_bytes=56 * 1024 * 1024
        ),
        cost_estimate=pl.CostEstimate(
            flops=2 * n * tok * q * width, bytes_accessed=2 * width * q, transcendentals=0
        ),
    )(dy, x, hidden.T, w, down.reshape(count * rank, width), up.reshape(count * rank, q), ads.T, live)
    out, dgrad, ugrad = pl.pallas_call(
        hand_over,
        out_shape=shapes,
        in_specs=[any_space] * 3,
        out_specs=(any_space,) * 3,
        scratch_shapes=[pltpu.VMEM(t.shape, t.dtype) for t in shapes] + [dma((12,)), dma((12,))],
    )(*results)
    return out, dgrad[None], ugrad[None]


def solution(mesh):
    n = mesh.shape["gx"]
    assert mesh.shape["gy"] == n
    placed = (
        P(("grp", "gx"), "gy"),
        P(("grp", "gy"), "gx"),
        P(("grp", "gx"), None),
        P("gx", "gy"),
        P("grp", None, "gx"),
        P("grp", None, "gy"),
        P(("grp", "gx"), None),
        P(("grp", "gx")),
    )
    return jax.shard_map(
        functools.partial(per_device, n),
        mesh=mesh,
        in_specs=placed,
        out_specs=(
            P(("grp", "gy"), "gx"),
            P(("grp", "gy"), None, "gx"),
            P(("grp", "gx"), None, "gy"),
        ),
        check_vma=False,
    )
```
